32 devices in a mesh: grp: 2 (over x), pool: 16 (over z, y, core).
Axes of the slice: x: 2, y: 2, z: 4, core: 2. Of those that a mesh axis runs over, the one named last changes fastest.
Arguments:
- queries: bfloat16 [32, 128, 1024], P(('grp', 'pool')), parts along dimension 0, may hold values from -400 to 400
- new_kv: bfloat16 [32, 128, 256], P(('grp', 'pool')), parts along dimension 0, may hold values from -16 to 16
- pool_kv: bfloat16 [64, 8, 128, 256], P(('grp', 'pool')), parts along dimension 0, may hold values from -16 to 16
- hit_slots: int32 [4, 16], P('grp'), parts along dimension 0, may hold values from 0 to 31, as said below
- prefix_blocks: int32 [4], P('grp'), parts along dimension 0, may hold values from 1 to 16, 20 in all
- new_owners: int32 [4, 2], P('grp'), parts along dimension 0, may hold values from 0 to 15, as said below
Outputs:
- attended: bfloat16 [32, 128, 1024], P(('grp', 'pool')), parts along dimension 0
- new_store: bfloat16 [32, 8, 128, 256], P(('grp', 'pool')), parts along dimension 0
The draws below stay inside these ranges and needn't reach their ends.
There are 2 independent parts, one for each index of `grp`. The reference program is written for one: setup_inputs(seed, part) draws one part's arguments, and reference() takes and returns one part's arrays. A program takes and returns all parts, laid end to end along the dimension named above; each array names one. Nothing has to cross between parts.
Inputs may be any that keep to these rules, and one draw needn't show every extreme that they name: `hit_slots`: slot s lies on owner s // 2. Block j of request r lies on owner (f + j) mod 16, where f depends on r and is a multiple of 4; one owner keeps different requests in different slots. Entries with j >= prefix_blocks[r] are unused. `prefix_blocks`: they sum to 20. `new_owners`: all 4 entries are distinct.
All inputs are finite; a program needn't handle non-finite values.
Results may differ from the reference program's by a relative error of at most 0.009.
Values may be sent and summed in bfloat16 or wider, within the bound.
A program may use at most 64 MiB of HBM per device.

```python
import math
import jax
import jax.numpy as jnp
import numpy as np
from jax import lax

HD = 128
KVH = 8
G = 8
BLK = 128
OWNERS = 16
REQS = 2
SLOTS = 2
MAXB = 16


def suffix_parts(key):
    base = jax.random.fold_in(key, 7)
    key_a, key_b, key_c = jax.random.split(base, 3)
    key_rows = jax.random.truncated_normal(key_a, -4.0, 4.0, (REQS * KVH, BLK, HD), jnp.float32)
    value_rows = 4.0 * jax.random.truncated_normal(key_b, -4.0, 4.0, (REQS * KVH, BLK, HD), jnp.float32)
    query_rows = 1.5 * jax.random.truncated_normal(key_c, -4.0, 4.0, (REQS * KVH, BLK, G, HD), jnp.float32)
    return (query_rows, key_rows, value_rows)


def draw_queries(key, part):
    query_rows, key_rows, value_rows = suffix_parts(key)
    return query_rows.reshape(REQS * KVH, BLK, G * HD).astype(jnp.bfloat16)


def draw_new_kv(key, part):
    query_rows, key_rows, value_rows = suffix_parts(key)
    return jnp.concatenate([key_rows, value_rows], 2).astype(jnp.bfloat16)


def draw_pool_kv(key, part):
    base = jax.random.fold_in(key, 13)
    shape = (OWNERS * SLOTS, KVH, BLK, 2 * HD)
    scales = jnp.concatenate([jnp.ones((HD,), jnp.float32), 4.0 * jnp.ones((HD,), jnp.float32)])
    raw = jax.random.truncated_normal(base, -4.0, 4.0, shape, jnp.float32)
    return (raw * scales).astype(jnp.bfloat16)


def draw_hit_slots(key, part):
    base = jax.random.fold_in(key, 17)
    key_a, key_b = jax.random.split(base)
    first_owner = 4 * jax.random.randint(key_a, (REQS,), 0, MAXB // 4)
    owner = (first_owner[:, None] + jnp.arange(MAXB)[None, :]) % MAXB
    orders = jax.vmap(lambda sub_key: jax.random.permutation(sub_key, SLOTS))(jax.random.split(key_b, MAXB))
    local_slot = orders[owner, jnp.arange(REQS)[:, None]]
    return (owner * SLOTS + local_slot).astype(jnp.int32)


def draw_new_owners(key, part):
    base = jax.random.fold_in(key, 19)
    chosen = jax.random.permutation(base, OWNERS)[:2 * REQS]
    return chosen.reshape(REQS, 2).astype(jnp.int32)


def profile(number_of, total, most, lean):
    portions = [(1 << 20) // math.isqrt(rank ** lean) + 1 for rank in range(2, number_of + 1)]
    spare, counts = total - most - (number_of - 1), [1] * (number_of - 1)
    while spare > 0:
        candidates = [i for i in range(number_of - 1) if counts[i] < most]
        mass, budget = sum([portions[i] for i in candidates]), spare
        for i in candidates:
            more = min(most - counts[i], max(1, budget * portions[i] // mass), spare)
            counts[i] = counts[i] + more
            spare = spare - more
    return np.array([most] + counts)


def uneven_parts(rng, amount, total, limit, slope):
    if amount == 2:
        one = jax.random.randint(rng, (), max(1, total - limit), min(limit, total - 1) + 1)
        return jnp.stack([one, total - one])
    lengths = jnp.asarray(profile(amount, total, limit, slope), jnp.int32)
    pairs = (amount - 1) // 2
    donor, taker = lengths[1:1 + 2 * pairs:2], lengths[2:2 + 2 * pairs:2]
    room = jnp.minimum(donor - 1, limit - taker)
    moved = jax.random.randint(jax.random.fold_in(rng, 1), (pairs,), 0, 1 << 20) % (room + 1)
    lengths = lengths.at[1:1 + 2 * pairs:2].set(donor - moved).at[2:2 + 2 * pairs:2].set(taker + moved)
    return lengths[jax.random.permutation(jax.random.fold_in(rng, 2), amount)]


def setup_inputs(seed: int = 0, part: int = 0) -> dict:
    seeds = jax.random.split(jax.random.key(seed), 7)
    part_splits = jax.random.split(jax.random.fold_in(seeds[6], part), 7)
    return {
        "queries": draw_queries(jax.random.fold_in(jax.random.fold_in(seeds[6], part), 71), part),
        "new_kv": draw_new_kv(jax.random.fold_in(jax.random.fold_in(seeds[6], part), 71), part),
        "pool_kv": draw_pool_kv(jax.random.fold_in(jax.random.fold_in(seeds[6], part), 71), part),
        "hit_slots": draw_hit_slots(jax.random.fold_in(jax.random.fold_in(seeds[6], part), 71), part),
        "prefix_blocks": uneven_parts(part_splits[4], REQS, 5 * REQS * MAXB // 8, MAXB, 2).astype(jnp.int32),
        "new_owners": draw_new_owners(jax.random.fold_in(jax.random.fold_in(seeds[6], part), 71), part),
    }


def reference(queries, new_kv, pool_kv, hit_slots, prefix_blocks, new_owners):
    score_scale = 1.0 / (HD ** 0.5)
    prefix_len = MAXB * BLK
    causal = jnp.arange(BLK)[None, :] <= jnp.arange(BLK)[:, None]

    def one_pair(pair_index):
        request = pair_index // KVH
        head = pair_index % KVH
        slots_used = hit_slots[request]
        cached = pool_kv[slots_used, head].reshape(prefix_len, 2 * HD)
        fresh = new_kv[pair_index]
        key_rows = jnp.concatenate([cached[:, :HD], fresh[:, :HD]], 0).astype(jnp.float32)
        value_rows = jnp.concatenate([cached[:, HD:], fresh[:, HD:]], 0).astype(jnp.float32)
        query_rows = queries[pair_index].reshape(BLK, G, HD).astype(jnp.float32)
        scores = jnp.einsum("tgd,kd->tgk", query_rows, key_rows) * score_scale
        in_prefix = jnp.arange(prefix_len) < prefix_blocks[request] * BLK
        usable = jnp.concatenate([jnp.broadcast_to(in_prefix[None, :], (BLK, prefix_len)), causal], 1)[:, None, :]
        scores = jnp.where(usable, scores, -jnp.inf)
        row_max = jnp.max(scores, axis=2, keepdims=True)
        weights = jnp.exp(scores - row_max)
        totals = jnp.sum(weights, axis=2)
        rounded = lax.optimization_barrier(weights.astype(jnp.bfloat16)).astype(jnp.float32)
        mixed = jnp.einsum("tgk,kd->tgd", rounded, value_rows) / totals[:, :, None]
        return mixed.reshape(BLK, G * HD).astype(jnp.bfloat16)

    attended = lax.map(one_pair, jnp.arange(REQS * KVH, dtype=jnp.int32))
    grouped = new_kv.reshape(REQS, KVH, BLK, 2 * HD)
    new_store = jnp.zeros((OWNERS, KVH, BLK, 2 * HD), jnp.bfloat16)
    new_store = new_store.at[new_owners[:, 0]].set(grouped).at[new_owners[:, 1]].set(grouped)
    return attended, new_store
```

```python
import functools
import math

import jax
import jax.numpy as jnp
from jax import lax
from jax.experimental import pallas as pl
from jax.experimental.pallas import tpu as pltpu
from jax.sharding import PartitionSpec as P

group_blocks = 4
column_chunk = 256
far_below = -1e30
far_above = 1e30
MESH = pl.DeviceIdType.MESH


def other(me, mask, n):
    out = 0
    bit = 1
    while bit < n:
        out = out + lax.rem(lax.div(me, bit) + (mask // bit if isinstance(mask, int) else lax.div(mask, bit)), 2) * bit
        bit *= 2
    return out


def kernel(
    n, hit_ref, prefix_ref, owner_ref, q_ref, new_ref, pool_ref, att_ref, store_ref,
    outgoing, fetched, gathered, chosen, rows, acc, top, total,
    send_sem, recv_sem, new_send, new_recv, pick_send, pick_recv,
):
    slots, heads, block, width = pool_ref.shape
    hd = width // 2
    requests, longest = hit_ref.shape
    groups = q_ref.shape[2] // hd
    columns = groups * block
    scale = math.log2(math.e) / math.sqrt(hd)
    me = lax.axis_index("pool")
    request, head = lax.div(me, heads), lax.rem(me, heads)

    barrier = pltpu.get_barrier_semaphore()
    for d in range(1, n):
        pl.semaphore_signal(barrier, inc=1, device_id={"pool": other(me, d, n)}, device_id_type=MESH)

    def first_owner(r):
        return lax.div(hit_ref[r, 0], slots)

    def stage(target):
        r, g = lax.div(target, heads), lax.rem(target, heads)
        place = lax.rem(me - first_owner(r) + n, n)
        slot = lax.rem(hit_ref[r, jnp.minimum(place, longest - 1)], slots)
        return pool_ref[slot, g]

    def block_copy(d):
        target = other(me, d, n)
        return pltpu.make_async_remote_copy(
            src_ref=outgoing.at[target], dst_ref=fetched.at[me],
            send_sem=send_sem.at[target], recv_sem=recv_sem.at[me],
            device_id={"pool": target}, device_id_type=MESH,
        )

    def block_arrival(source):
        return pltpu.make_async_remote_copy(
            src_ref=outgoing.at[source], dst_ref=fetched.at[source],
            send_sem=send_sem.at[source], recv_sem=recv_sem.at[source],
            device_id={"pool": source}, device_id_type=MESH,
        )

    def new_copy(i):
        target = other(me, i * heads, n)
        return pltpu.make_async_remote_copy(
            src_ref=new_ref.at[0], dst_ref=gathered.at[request],
            send_sem=new_send.at[i], recv_sem=new_recv.at[request],
            device_id={"pool": target}, device_id_type=MESH,
        )

    def new_arrival(i):
        target = other(me, i * heads, n)
        r = lax.div(target, heads)
        return pltpu.make_async_remote_copy(
            src_ref=new_ref.at[0], dst_ref=gathered.at[r],
            send_sem=new_send.at[i], recv_sem=new_recv.at[r],
            device_id={"pool": target}, device_id_type=MESH,
        )

    def pick_copy(i, place):
        target = other(me, i, n)
        return pltpu.make_async_remote_copy(
            src_ref=chosen.at[i], dst_ref=store_ref.at[0, place],
            send_sem=pick_send.at[i], recv_sem=pick_recv.at[place],
            device_id={"pool": target}, device_id_type=MESH,
        )

    def pick(target):
        source, owned = 0, 0
        for r in range(requests):
            here = jnp.where((owner_ref[r, 0] == target) | (owner_ref[r, 1] == target), 1, 0)
            source = source + r * here
            owned = owned + here
        value = gathered[source]
        return jnp.where(owned > 0, value, jnp.zeros_like(value))

    order = []
    for i in range(n // 2):
        order += [n // 2 + i] + ([i + 1] if i + 1 < n // 2 else [])
    for d in order:
        target = other(me, d, n)
        outgoing[target] = stage(target)
    fetched[me] = stage(me)
    gathered[request] = new_ref[0]
    for h in range(groups):
        rows[h * block:(h + 1) * block, :] = q_ref[0, :, h * hd:(h + 1) * hd]
    pl.semaphore_wait(barrier, n - 1)

    for i in range(1, requests):
        new_copy(i).start()
    for d in order:
        block_copy(d).start()

    own_keys, own_values = new_ref[0, :, :hd], new_ref[0, :, hd:].T
    for c in range(0, columns, column_chunk):
        span = slice(c, c + column_chunk)
        s = lax.dot_general(
            own_keys, rows[span, :], (((1,), (1,)), ((), ())), preferred_element_type=jnp.float32
        ) * scale
        key_at = lax.broadcasted_iota(jnp.int32, s.shape, 0)
        token_at = lax.rem(lax.broadcasted_iota(jnp.int32, s.shape, 1), block)
        s = jnp.where(key_at <= token_at, s, far_below)
        m = jnp.max(s, axis=0, keepdims=True)
        w = jnp.where(key_at <= token_at, jnp.exp2(s - m), 0.0)
        top[:, span] = m
        total[:, span] = jnp.sum(w, axis=0, keepdims=True)
        acc[:, span] = jnp.dot(own_values, w.astype(jnp.bfloat16), preferred_element_type=jnp.float32)

    begin = first_owner(request)
    length = prefix_ref[0, request]

    def fold(base):
        stored = fetched.at[pl.ds(base, group_blocks)]
        keys = stored[:, :, :hd].reshape(group_blocks * block, hd)
        values = stored[:, :, hd:].reshape(group_blocks * block, hd).T
        live = [lax.rem(base + j - begin + n, n) < length for j in range(group_blocks)]
        for c in range(0, columns, column_chunk):
            span = slice(c, c + column_chunk)
            s = lax.dot_general(
                keys, rows[span, :], (((1,), (1,)), ((), ())), preferred_element_type=jnp.float32
            ) * scale
            before = top[:, span]
            m = before
            for j in range(group_blocks):
                peak = jnp.max(s[j * block:(j + 1) * block], axis=0, keepdims=True)
                m = jnp.maximum(m, jnp.where(live[j], peak, far_below))
            factor = jnp.exp2(before - m)
            parts = [
                jnp.exp2(s[j * block:(j + 1) * block] - jnp.where(live[j], m, far_above))
                for j in range(group_blocks)
            ]
            w = jnp.concatenate(parts, axis=0)
            top[:, span] = m
            total[:, span] = total[:, span] * factor + jnp.sum(w, axis=0, keepdims=True)
            acc[:, span] = acc[:, span] * factor + jnp.dot(
                values, w.astype(jnp.bfloat16), preferred_element_type=jnp.float32
            )

    for i in range(1, requests):
        new_arrival(i).wait_recv()
    for i in range(1, heads):
        chosen[i] = pick(other(me, i, n))
        pick_copy(i, head).start()
    store_ref[0, head] = pick(me)

    for d in range(1, group_blocks):
        block_arrival(other(me, d, n)).wait_recv()
    fold(lax.div(me, group_blocks) * group_blocks)

    @pl.loop(1, n // group_blocks)
    def _(i):
        base = other(lax.div(me, group_blocks), i, n // group_blocks) * group_blocks
        for j in range(group_blocks):
            block_arrival(base + j).wait_recv()
        fold(base)

    for h in range(groups):
        span = slice(h * block, (h + 1) * block)
        att_ref[0, :, h * hd:(h + 1) * hd] = (acc[:, span] / total[:, span]).T.astype(att_ref.dtype)

    for i in range(1, heads):
        pick_copy(i, lax.rem(other(me, i, n), heads)).wait_recv()
    for i in range(1, heads):
        pick_copy(i, head).wait_send()
    for i in range(1, requests):
        new_copy(i).wait_send()
    for d in order:
        block_copy(d).wait_send()


def on_device(n, queries, new_kv, pool_kv, hit_slots, prefix_blocks, new_owners):
    heads, block, width = pool_kv.shape[1:]
    requests = hit_slots.shape[0]
    hd = width // 2
    columns = queries.shape[2] // hd * block
    smem, vmem = pl.BlockSpec(memory_space=pltpu.SMEM), pl.BlockSpec(memory_space=pltpu.VMEM)
    slab = lambda k: pltpu.VMEM((k, block, width), pool_kv.dtype)
    dma = lambda k: pltpu.SemaphoreType.DMA((k,))
    keys = (n + 1) * block
    return pl.pallas_call(
        functools.partial(kernel, n),
        out_shape=(
            jax.ShapeDtypeStruct(queries.shape, queries.dtype),
            jax.ShapeDtypeStruct((1, heads, block, width), pool_kv.dtype),
        ),
        in_specs=[smem] * 3 + [vmem] * 3,
        out_specs=(vmem, vmem),
        scratch_shapes=[
            slab(n), slab(n), slab(requests), slab(heads),
            pltpu.VMEM((columns, hd), jnp.bfloat16),
            pltpu.VMEM((hd, columns), jnp.float32),
            pltpu.VMEM((1, columns), jnp.float32),
            pltpu.VMEM((1, columns), jnp.float32),
            dma(n), dma(n), dma(requests), dma(requests), dma(heads), dma(heads),
        ],
        compiler_params=pltpu.CompilerParams(
            collective_id=0, has_side_effects=True, vmem_limit_bytes=48 * 2**20
        ),
        cost_estimate=pl.CostEstimate(
            flops=4 * columns * keys * hd,
            bytes_accessed=2 * (pool_kv.size + 2 * queries.size + 2 * heads * block * width),
            transcendentals=columns * keys,
        ),
    )(hit_slots, prefix_blocks[None], new_owners, queries, new_kv, pool_kv)


def solution(mesh):
    placed = (
        P(("grp", "pool"), None, None),
        P(("grp", "pool"), None, None),
        P(("grp", "pool"), None, None, None),
        P("grp", None),
        P("grp"),
        P("grp", None),
    )
    return jax.shard_map(
        functools.partial(on_device, mesh.shape["pool"]),
        mesh=mesh,
        in_specs=placed,
        out_specs=(P(("grp", "pool"), None, None), P(("grp", "pool"), None, None, None)),
        check_vma=False,
    )
```

```python
import functools
import math

import jax
import jax.numpy as jnp
from jax import lax
from jax.experimental import pallas as pl
from jax.experimental.pallas import tpu as pltpu
from jax.sharding import PartitionSpec as P

group_blocks = 4
column_chunk = 256
far_below = -1e30
far_above = 1e30
MESH = pl.DeviceIdType.MESH


def other(me, mask, n):
    out = 0
    bit = 1
    while bit < n:
        out = out + lax.rem(lax.div(me, bit) + (mask // bit if isinstance(mask, int) else lax.div(mask, bit)), 2) * bit
        bit *= 2
    return out


def kernel(
    n, hit_hbm, prefix_hbm, owner_hbm, q_hbm, new_hbm, pool_hbm, att_ref, store_ref,
    hit_ref, prefix_ref, owner_ref, q_ref, new_ref, pool_ref, in_sem, outgoing, fetched, gathered, chosen, rows, acc, top, total,
    send_sem, recv_sem, new_send, new_recv, pick_send, pick_recv,
):
    slots, heads, block, width = pool_ref.shape
    hd = width // 2
    requests, longest = hit_ref.shape
    groups = q_ref.shape[2] // hd
    columns = groups * block
    scale = math.log2(math.e) / math.sqrt(hd)
    me = lax.axis_index("pool")
    request, head = lax.div(me, heads), lax.rem(me, heads)

    loads = [
        pltpu.make_async_copy(hit_hbm, hit_ref, in_sem.at[0]),
        pltpu.make_async_copy(prefix_hbm, prefix_ref, in_sem.at[1]),
        pltpu.make_async_copy(owner_hbm, owner_ref, in_sem.at[2]),
        pltpu.make_async_copy(new_hbm, new_ref, in_sem.at[3]),
        pltpu.make_async_copy(q_hbm, q_ref, in_sem.at[4]),
    ] + [
        pltpu.make_async_copy(pool_hbm.at[k], pool_ref.at[k], in_sem.at[5 + k]) for k in range(slots)
    ]
    for load in loads:
        load.start()
    barrier = pltpu.get_barrier_semaphore()
    for d in range(1, n):
        pl.semaphore_signal(barrier, inc=1, device_id={"pool": other(me, d, n)}, device_id_type=MESH)

    def first_owner(r):
        return lax.div(hit_ref[r, 0], slots)

    def stage(target):
        r, g = lax.div(target, heads), lax.rem(target, heads)
        place = lax.rem(me - first_owner(r) + n, n)
        slot = lax.rem(hit_ref[r, jnp.minimum(place, longest - 1)], slots)
        return pool_ref[slot, g]

    def block_copy(d):
        target = other(me, d, n)
        return pltpu.make_async_remote_copy(
            src_ref=outgoing.at[target], dst_ref=fetched.at[me],
            send_sem=send_sem.at[target], recv_sem=recv_sem.at[me],
            device_id={"pool": target}, device_id_type=MESH,
        )

    def block_arrival(source):
        return pltpu.make_async_remote_copy(
            src_ref=outgoing.at[source], dst_ref=fetched.at[source],
            send_sem=send_sem.at[source], recv_sem=recv_sem.at[source],
            device_id={"pool": source}, device_id_type=MESH,
        )

    def new_copy(i):
        target = other(me, i * heads, n)
        return pltpu.make_async_remote_copy(
            src_ref=new_ref.at[0], dst_ref=gathered.at[request],
            send_sem=new_send.at[i], recv_sem=new_recv.at[request],
            device_id={"pool": target}, device_id_type=MESH,
        )

    def new_arrival(i):
        target = other(me, i * heads, n)
        r = lax.div(target, heads)
        return pltpu.make_async_remote_copy(
            src_ref=new_ref.at[0], dst_ref=gathered.at[r],
            send_sem=new_send.at[i], recv_sem=new_recv.at[r],
            device_id={"pool": target}, device_id_type=MESH,
        )

    def pick_copy(i, place):
        target = other(me, i, n)
        return pltpu.make_async_remote_copy(
            src_ref=chosen.at[i], dst_ref=store_ref.at[0, place],
            send_sem=pick_send.at[i], recv_sem=pick_recv.at[place],
            device_id={"pool": target}, device_id_type=MESH,
        )

    def pick(target):
        source, owned = 0, 0
        for r in range(requests):
            here = jnp.where((owner_ref[r, 0] == target) | (owner_ref[r, 1] == target), 1, 0)
            source = source + r * here
            owned = owned + here
        value = gathered[source]
        return jnp.where(owned > 0, value, jnp.zeros_like(value))

    for load in loads:
        load.wait()
    order = []
    for i in range(n // 2):
        order += [n // 2 + i] + ([i + 1] if i + 1 < n // 2 else [])
    for d in order:
        target = other(me, d, n)
        outgoing[target] = stage(target)
    fetched[me] = stage(me)
    gathered[request] = new_ref[0]
    for h in range(groups):
        rows[h * block:(h + 1) * block, :] = q_ref[0, :, h * hd:(h + 1) * hd]
    pl.semaphore_wait(barrier, n - 1)

    for i in range(1, requests):
        new_copy(i).start()
    for d in order:
        block_copy(d).start()

    own_keys, own_values = new_ref[0, :, :hd], new_ref[0, :, hd:].T
    for c in range(0, columns, column_chunk):
        span = slice(c, c + column_chunk)
        s = lax.dot_general(
            own_keys, rows[span, :], (((1,), (1,)), ((), ())), preferred_element_type=jnp.float32
        ) * scale
        key_at = lax.broadcasted_iota(jnp.int32, s.shape, 0)
        token_at = lax.rem(lax.broadcasted_iota(jnp.int32, s.shape, 1), block)
        s = jnp.where(key_at <= token_at, s, far_below)
        m = jnp.max(s, axis=0, keepdims=True)
        w = jnp.where(key_at <= token_at, jnp.exp2(s - m), 0.0)
        top[:, span] = m
        total[:, span] = jnp.sum(w, axis=0, keepdims=True)
        acc[:, span] = jnp.dot(own_values, w.astype(jnp.bfloat16), preferred_element_type=jnp.float32)

    begin = first_owner(request)
    length = prefix_ref[0, request]

    def fold(base):
        stored = fetched.at[pl.ds(base, group_blocks)]
        keys = stored[:, :, :hd].reshape(group_blocks * block, hd)
        values = stored[:, :, hd:].reshape(group_blocks * block, hd).T
        live = [lax.rem(base + j - begin + n, n) < length for j in range(group_blocks)]
        for c in range(0, columns, column_chunk):
            span = slice(c, c + column_chunk)
            s = lax.dot_general(
                keys, rows[span, :], (((1,), (1,)), ((), ())), preferred_element_type=jnp.float32
            ) * scale
            before = top[:, span]
            m = before
            for j in range(group_blocks):
                peak = jnp.max(s[j * block:(j + 1) * block], axis=0, keepdims=True)
                m = jnp.maximum(m, jnp.where(live[j], peak, far_below))
            factor = jnp.exp2(before - m)
            parts = [
                jnp.exp2(s[j * block:(j + 1) * block] - jnp.where(live[j], m, far_above))
                for j in range(group_blocks)
            ]
            w = jnp.concatenate(parts, axis=0)
            top[:, span] = m
            total[:, span] = total[:, span] * factor + jnp.sum(w, axis=0, keepdims=True)
            acc[:, span] = acc[:, span] * factor + jnp.dot(
                values, w.astype(jnp.bfloat16), preferred_element_type=jnp.float32
            )

    for i in range(1, requests):
        new_arrival(i).wait_recv()
    for i in range(1, heads):
        chosen[i] = pick(other(me, i, n))
        pick_copy(i, head).start()
    store_ref[0, head] = pick(me)

    for d in range(1, group_blocks):
        block_arrival(other(me, d, n)).wait_recv()
    fold(lax.div(me, group_blocks) * group_blocks)

    @pl.loop(1, n // group_blocks)
    def _(i):
        base = other(lax.div(me, group_blocks), i, n // group_blocks) * group_blocks
        for j in range(group_blocks):
            block_arrival(base + j).wait_recv()
        fold(base)

    for h in range(groups):
        span = slice(h * block, (h + 1) * block)
        att_ref[0, :, h * hd:(h + 1) * hd] = (acc[:, span] / total[:, span]).T.astype(att_ref.dtype)

    for i in range(1, heads):
        pick_copy(i, lax.rem(other(me, i, n), heads)).wait_recv()
    for i in range(1, heads):
        pick_copy(i, head).wait_send()
    for i in range(1, requests):
        new_copy(i).wait_send()
    for d in order:
        block_copy(d).wait_send()


def on_device(n, queries, new_kv, pool_kv, hit_slots, prefix_blocks, new_owners):
    heads, block, width = pool_kv.shape[1:]
    requests = hit_slots.shape[0]
    hd = width // 2
    columns = queries.shape[2] // hd * block
    hbm, vmem = pl.BlockSpec(memory_space=pltpu.HBM), pl.BlockSpec(memory_space=pltpu.VMEM)
    slab = lambda k: pltpu.VMEM((k, block, width), pool_kv.dtype)
    dma = lambda k: pltpu.SemaphoreType.DMA((k,))
    keys = (n + 1) * block
    return pl.pallas_call(
        functools.partial(kernel, n),
        out_shape=(
            jax.ShapeDtypeStruct(queries.shape, queries.dtype),
            jax.ShapeDtypeStruct((1, heads, block, width), pool_kv.dtype),
        ),
        in_specs=[hbm] * 6,
        out_specs=(vmem, vmem),
        scratch_shapes=[
            pltpu.SMEM(hit_slots.shape, jnp.int32), pltpu.SMEM((1, requests), jnp.int32),
            pltpu.SMEM(new_owners.shape, jnp.int32),
            pltpu.VMEM(queries.shape, queries.dtype), pltpu.VMEM(new_kv.shape, new_kv.dtype),
            pltpu.VMEM(pool_kv.shape, pool_kv.dtype), dma(5 + pool_kv.shape[0]),
            slab(n), slab(n), slab(requests), slab(heads),
            pltpu.VMEM((columns, hd), jnp.bfloat16),
            pltpu.VMEM((hd, columns), jnp.float32),
            pltpu.VMEM((1, columns), jnp.float32),
            pltpu.VMEM((1, columns), jnp.float32),
            dma(n), dma(n), dma(requests), dma(requests), dma(heads), dma(heads),
        ],
        compiler_params=pltpu.CompilerParams(
            collective_id=0, has_side_effects=True, vmem_limit_bytes=48 * 2**20
        ),
        cost_estimate=pl.CostEstimate(
            flops=4 * columns * keys * hd,
            bytes_accessed=2 * (pool_kv.size + 2 * queries.size + 2 * heads * block * width),
            transcendentals=columns * keys,
        ),
    )(hit_slots, prefix_blocks[None], new_owners, queries, new_kv, pool_kv)


def solution(mesh):
    placed = (
        P(("grp", "pool"), None, None),
        P(("grp", "pool"), None, None),
        P(("grp", "pool"), None, None, None),
        P("grp", None),
        P("grp"),
        P("grp", None),
    )
    return jax.shard_map(
        functools.partial(on_device, mesh.shape["pool"]),
        mesh=mesh,
        in_specs=placed,
        out_specs=(P(("grp", "pool"), None, None), P(("grp", "pool"), None, None, None)),
        check_vma=False,
    )
```

```python
import functools
import math

import jax
import jax.numpy as jnp
from jax import lax
from jax.experimental import pallas as pl
from jax.experimental.pallas import tpu as pltpu
from jax.sharding import PartitionSpec as P

group_blocks = 4
column_chunk = 256
far_below = -1e30
far_above = 1e30
MESH = pl.DeviceIdType.MESH


def other(me, mask, n):
    out = 0
    bit = 1
    while bit < n:
        out = out + lax.rem(lax.div(me, bit) + (mask // bit if isinstance(mask, int) else lax.div(mask, bit)), 2) * bit
        bit *= 2
    return out


def kernel(
    n, hit_hbm, prefix_hbm, owner_hbm, q_hbm, new_hbm, pool_hbm, att_ref, store_ref,
    hit_ref, prefix_ref, owner_ref, q_ref, new_ref, pool_ref, in_sem, outgoing, fetched, gathered, chosen, rows, acc, top, total,
    send_sem, recv_sem, new_send, new_recv, pick_send, pick_recv,
):
    slots, heads, block, width = pool_ref.shape
    hd = width // 2
    requests, longest = hit_ref.shape
    groups = q_ref.shape[2] // hd
    columns = groups * block
    scale = math.log2(math.e) / math.sqrt(hd)
    me = lax.axis_index("pool")
    request, head = lax.div(me, heads), lax.rem(me, heads)

    loads = [
        pltpu.make_async_copy(hit_hbm, hit_ref, in_sem.at[0]),
        pltpu.make_async_copy(prefix_hbm, prefix_ref, in_sem.at[1]),
        pltpu.make_async_copy(owner_hbm, owner_ref, in_sem.at[2]),
        pltpu.make_async_copy(new_hbm, new_ref, in_sem.at[3]),
        pltpu.make_async_copy(q_hbm, q_ref, in_sem.at[4]),
    ] + [
        pltpu.make_async_copy(pool_hbm.at[k], pool_ref.at[k], in_sem.at[5 + k]) for k in range(slots)
    ]
    for load in loads:
        load.start()
    barrier = pltpu.get_barrier_semaphore()
    for d in range(1, n):
        pl.semaphore_signal(barrier, inc=1, device_id={"pool": other(me, d, n)}, device_id_type=MESH)

    def first_owner(r):
        return lax.div(hit_ref[r, 0], slots)

    def stage(target):
        r, g = lax.div(target, heads), lax.rem(target, heads)
        place = lax.rem(me - first_owner(r) + n, n)
        slot = lax.rem(hit_ref[r, jnp.minimum(place, longest - 1)], slots)
        return pool_ref[slot, g]

    def block_copy(d):
        target = other(me, d, n)
        return pltpu.make_async_remote_copy(
            src_ref=outgoing.at[target], dst_ref=fetched.at[me],
            send_sem=send_sem.at[target], recv_sem=recv_sem.at[me],
            device_id={"pool": target}, device_id_type=MESH,
        )

    def block_arrival(source):
        return pltpu.make_async_remote_copy(
            src_ref=outgoing.at[source], dst_ref=fetched.at[source],
            send_sem=send_sem.at[source], recv_sem=recv_sem.at[source],
            device_id={"pool": source}, device_id_type=MESH,
        )

    def new_copy(i):
        target = other(me, i * heads, n)
        return pltpu.make_async_remote_copy(
            src_ref=new_ref.at[0], dst_ref=gathered.at[request],
            send_sem=new_send.at[i], recv_sem=new_recv.at[request],
            device_id={"pool": target}, device_id_type=MESH,
        )

    def new_arrival(i):
        target = other(me, i * heads, n)
        r = lax.div(target, heads)
        return pltpu.make_async_remote_copy(
            src_ref=new_ref.at[0], dst_ref=gathered.at[r],
            send_sem=new_send.at[i], recv_sem=new_recv.at[r],
            device_id={"pool": target}, device_id_type=MESH,
        )

    def pick_copy(i, place):
        target = other(me, i, n)
        return pltpu.make_async_remote_copy(
            src_ref=chosen.at[i], dst_ref=store_ref.at[0, place],
            send_sem=pick_send.at[i], recv_sem=pick_recv.at[place],
            device_id={"pool": target}, device_id_type=MESH,
        )

    def pick(target):
        source, owned = 0, 0
        for r in range(requests):
            here = jnp.where((owner_ref[r, 0] == target) | (owner_ref[r, 1] == target), 1, 0)
            source = source + r * here
            owned = owned + here
        value = gathered[source]
        return jnp.where(owned > 0, value, jnp.zeros_like(value))

    for load in loads:
        load.wait()
    order = []
    for i in range(n // 2):
        order += [n // 2 + i] + ([i + 1] if i + 1 < n // 2 else [])
    for d in order:
        target = other(me, d, n)
        outgoing[target] = stage(target)
    fetched[me] = stage(me)
    gathered[request] = new_ref[0]
    for h in range(groups):
        rows[h * block:(h + 1) * block, :] = q_ref[0, :, h * hd:(h + 1) * hd]
    pl.semaphore_wait(barrier, n - 1)

    for i in range(1, requests):
        new_copy(i).start()
    for d in order:
        block_copy(d).start()

    own_keys, own_values = new_ref[0, :, :hd], new_ref[0, :, hd:].T
    for c in range(0, columns, column_chunk):
        span = slice(c, c + column_chunk)
        s = lax.dot_general(
            own_keys, rows[span, :], (((1,), (1,)), ((), ())), preferred_element_type=jnp.float32
        ) * scale
        key_at = lax.broadcasted_iota(jnp.int32, s.shape, 0)
        token_at = lax.rem(lax.broadcasted_iota(jnp.int32, s.shape, 1), block)
        s = jnp.where(key_at <= token_at, s, far_below)
        m = jnp.max(s, axis=0, keepdims=True)
        w = jnp.where(key_at <= token_at, jnp.exp2(s - m), 0.0)
        top[:, span] = m
        total[:, span] = jnp.sum(w, axis=0, keepdims=True)
        acc[:, span] = jnp.dot(own_values, w.astype(jnp.bfloat16), preferred_element_type=jnp.float32)

    begin = first_owner(request)
    length = prefix_ref[0, request]

    def fold(base):
        stored = fetched.at[pl.ds(base, group_blocks)]
        keys = stored[:, :, :hd].reshape(group_blocks * block, hd)
        values = stored[:, :, hd:].reshape(group_blocks * block, hd).T
        live = [lax.rem(base + j - begin + n, n) < length for j in range(group_blocks)]
        for c in range(0, columns, column_chunk):
            span = slice(c, c + column_chunk)
            s = lax.dot_general(
                keys, rows[span, :], (((1,), (1,)), ((), ())), preferred_element_type=jnp.float32
            ) * scale
            before = top[:, span]
            m = before
            for j in range(group_blocks):
                peak = jnp.max(s[j * block:(j + 1) * block], axis=0, keepdims=True)
                m = jnp.maximum(m, jnp.where(live[j], peak, far_below))
            factor = jnp.exp2(before - m)
            parts = [
                jnp.exp2(s[j * block:(j + 1) * block] - jnp.where(live[j], m, far_above))
                for j in range(group_blocks)
            ]
            w = jnp.concatenate(parts, axis=0)
            top[:, span] = m
            total[:, span] = total[:, span] * factor + jnp.sum(w, axis=0, keepdims=True)
            acc[:, span] = acc[:, span] * factor + jnp.dot(
                values, w.astype(jnp.bfloat16), preferred_element_type=jnp.float32
            )

    for i in range(1, requests):
        new_arrival(i).wait_recv()
    for i in range(1, heads):
        chosen[i] = pick(other(me, i, n))
        pick_copy(i, head).start()
    store_ref[0, head] = pick(me)

    for d in range(1, group_blocks):
        block_arrival(other(me, d, n)).wait_recv()
    fold(lax.div(me, group_blocks) * group_blocks)

    @pl.loop(1, n // group_blocks)
    def _(i):
        base = other(lax.div(me, group_blocks), i, n // group_blocks) * group_blocks
        for j in range(group_blocks):
            block_arrival(base + j).wait_recv()
        fold(base)

    for h in range(groups):
        span = slice(h * block, (h + 1) * block)
        att_ref[0, :, h * hd:(h + 1) * hd] = (acc[:, span] / total[:, span]).T.astype(att_ref.dtype)

    for i in range(1, heads):
        pick_copy(i, lax.rem(other(me, i, n), heads)).wait_recv()
    for i in range(1, heads):
        pick_copy(i, head).wait_send()
    for i in range(1, requests):
        new_copy(i).wait_send()
    for d in order:
        block_copy(d).wait_send()


def on_device(n, queries, new_kv, pool_kv, hit_slots, prefix_blocks, new_owners):
    heads, block, width = pool_kv.shape[1:]
    requests = hit_slots.shape[0]
    hd = width // 2
    columns = queries.shape[2] // hd * block
    hbm, vmem = pl.BlockSpec(memory_space=pltpu.HBM), pl.BlockSpec(memory_space=pltpu.VMEM)
    slab = lambda k: pltpu.VMEM((k, block, width), pool_kv.dtype)
    dma = lambda k: pltpu.SemaphoreType.DMA((k,))
    keys = (n + 1) * block
    return pl.pallas_call(
        functools.partial(kernel, n),
        out_shape=(
            jax.ShapeDtypeStruct(queries.shape, queries.dtype),
            jax.ShapeDtypeStruct((1, heads, block, width), pool_kv.dtype),
        ),
        in_specs=[hbm] * 6,
        out_specs=(vmem, vmem),
        scratch_shapes=[
            pltpu.SMEM(hit_slots.shape, jnp.int32), pltpu.SMEM((1, requests), jnp.int32),
            pltpu.SMEM(new_owners.shape, jnp.int32),
            pltpu.VMEM(queries.shape, queries.dtype), pltpu.VMEM(new_kv.shape, new_kv.dtype),
            pltpu.VMEM(pool_kv.shape, pool_kv.dtype), dma(5 + pool_kv.shape[0]),
            slab(n), slab(n), slab(requests), slab(heads),
            pltpu.VMEM((columns, hd), jnp.bfloat16),
            pltpu.VMEM((hd, columns), jnp.float32),
            pltpu.VMEM((1, columns), jnp.float32),
            pltpu.VMEM((1, columns), jnp.float32),
            dma(n), dma(n), dma(requests), dma(requests), dma(heads), dma(heads),
        ],
        compiler_params=pltpu.CompilerParams(
            collective_id=0, has_side_effects=True, vmem_limit_bytes=56 * 2**20
        ),
        cost_estimate=pl.CostEstimate(
            flops=4 * columns * keys * hd,
            bytes_accessed=2 * (pool_kv.size + 2 * queries.size + 2 * heads * block * width),
            transcendentals=columns * keys,
        ),
    )(hit_slots, prefix_blocks[None], new_owners, queries, new_kv, pool_kv)


def solution(mesh):
    placed = (
        P(("grp", "pool"), None, None),
        P(("grp", "pool"), None, None),
        P(("grp", "pool"), None, None, None),
        P("grp", None),
        P("grp"),
        P("grp", None),
    )
    return jax.shard_map(
        functools.partial(on_device, mesh.shape["pool"]),
        mesh=mesh,
        in_specs=placed,
        out_specs=(P(("grp", "pool"), None, None), P(("grp", "pool"), None, None, None)),
        check_vma=False,
    )
```

```python
import functools
import math

import jax
import jax.numpy as jnp
from jax import lax
from jax.experimental import pallas as pl
from jax.experimental.pallas import tpu as pltpu
from jax.sharding import PartitionSpec as P

group_blocks = 2
column_chunk = 256
far_below = -1e30
far_above = 1e30
MESH = pl.DeviceIdType.MESH


def other(me, mask, n):
    out = 0
    bit = 1
    while bit < n:
        out = out + lax.rem(lax.div(me, bit) + (mask // bit if isinstance(mask, int) else lax.div(mask, bit)), 2) * bit
        bit *= 2
    return out


def kernel(
    n, hit_hbm, prefix_hbm, owner_hbm, q_hbm, new_hbm, pool_hbm, att_ref, store_ref,
    hit_ref, prefix_ref, owner_ref, q_ref, new_ref, pool_ref, in_sem, outgoing, fetched, gathered, chosen, rows, acc, top, total,
    send_sem, recv_sem, new_send, new_recv, pick_send, pick_recv,
):
    slots, heads, block, width = pool_ref.shape
    hd = width // 2
    requests, longest = hit_ref.shape
    groups = q_ref.shape[2] // hd
    columns = groups * block
    scale = math.log2(math.e) / math.sqrt(hd)
    me = lax.axis_index("pool")
    request, head = lax.div(me, heads), lax.rem(me, heads)

    loads = [
        pltpu.make_async_copy(hit_hbm, hit_ref, in_sem.at[0]),
        pltpu.make_async_copy(prefix_hbm, prefix_ref, in_sem.at[1]),
        pltpu.make_async_copy(owner_hbm, owner_ref, in_sem.at[2]),
        pltpu.make_async_copy(new_hbm, new_ref, in_sem.at[3]),
        pltpu.make_async_copy(q_hbm, q_ref, in_sem.at[4]),
    ] + [
        pltpu.make_async_copy(pool_hbm.at[k], pool_ref.at[k], in_sem.at[5 + k]) for k in range(slots)
    ]
    for load in loads:
        load.start()
    barrier = pltpu.get_barrier_semaphore()
    for d in range(1, n):
        pl.semaphore_signal(barrier, inc=1, device_id={"pool": other(me, d, n)}, device_id_type=MESH)

    def first_owner(r):
        return lax.div(hit_ref[r, 0], slots)

    def stage(target):
        r, g = lax.div(target, heads), lax.rem(target, heads)
        place = lax.rem(me - first_owner(r) + n, n)
        slot = lax.rem(hit_ref[r, jnp.minimum(place, longest - 1)], slots)
        return pool_ref[slot, g]

    def block_copy(d):
        target = other(me, d, n)
        return pltpu.make_async_remote_copy(
            src_ref=outgoing.at[target], dst_ref=fetched.at[me],
            send_sem=send_sem.at[target], recv_sem=recv_sem.at[me],
            device_id={"pool": target}, device_id_type=MESH,
        )

    def block_arrival(source):
        return pltpu.make_async_remote_copy(
            src_ref=outgoing.at[source], dst_ref=fetched.at[source],
            send_sem=send_sem.at[source], recv_sem=recv_sem.at[source],
            device_id={"pool": source}, device_id_type=MESH,
        )

    def new_copy(i):
        target = other(me, i * heads, n)
        return pltpu.make_async_remote_copy(
            src_ref=new_ref.at[0], dst_ref=gathered.at[request],
            send_sem=new_send.at[i], recv_sem=new_recv.at[request],
            device_id={"pool": target}, device_id_type=MESH,
        )

    def new_arrival(i):
        target = other(me, i * heads, n)
        r = lax.div(target, heads)
        return pltpu.make_async_remote_copy(
            src_ref=new_ref.at[0], dst_ref=gathered.at[r],
            send_sem=new_send.at[i], recv_sem=new_recv.at[r],
            device_id={"pool": target}, device_id_type=MESH,
        )

    def pick_copy(i, place):
        target = other(me, i, n)
        return pltpu.make_async_remote_copy(
            src_ref=chosen.at[i], dst_ref=store_ref.at[0, place],
            send_sem=pick_send.at[i], recv_sem=pick_recv.at[place],
            device_id={"pool": target}, device_id_type=MESH,
        )

    def pick(target):
        source, owned = 0, 0
        for r in range(requests):
            here = jnp.where((owner_ref[r, 0] == target) | (owner_ref[r, 1] == target), 1, 0)
            source = source + r * here
            owned = owned + here
        value = gathered[source]
        return jnp.where(owned > 0, value, jnp.zeros_like(value))

    for load in loads:
        load.wait()
    order = []
    for i in range(n // 2):
        order += [n // 2 + i] + ([i + 1] if i + 1 < n // 2 else [])
    for d in order:
        target = other(me, d, n)
        outgoing[target] = stage(target)
    fetched[me] = stage(me)
    gathered[request] = new_ref[0]
    for h in range(groups):
        rows[h * block:(h + 1) * block, :] = q_ref[0, :, h * hd:(h + 1) * hd]
    pl.semaphore_wait(barrier, n - 1)

    for i in range(1, requests):
        new_copy(i).start()
    for d in order:
        block_copy(d).start()

    own_keys, own_values = new_ref[0, :, :hd], new_ref[0, :, hd:].T
    for c in range(0, columns, column_chunk):
        span = slice(c, c + column_chunk)
        s = lax.dot_general(
            own_keys, rows[span, :], (((1,), (1,)), ((), ())), preferred_element_type=jnp.float32
        ) * scale
        key_at = lax.broadcasted_iota(jnp.int32, s.shape, 0)
        token_at = lax.rem(lax.broadcasted_iota(jnp.int32, s.shape, 1), block)
        s = jnp.where(key_at <= token_at, s, far_below)
        m = jnp.max(s, axis=0, keepdims=True)
        w = jnp.where(key_at <= token_at, jnp.exp2(s - m), 0.0)
        top[:, span] = m
        total[:, span] = jnp.sum(w, axis=0, keepdims=True)
        acc[:, span] = jnp.dot(own_values, w.astype(jnp.bfloat16), preferred_element_type=jnp.float32)

    begin = first_owner(request)
    length = prefix_ref[0, request]

    def fold(base):
        stored = fetched.at[pl.ds(base, group_blocks)]
        keys = stored[:, :, :hd].reshape(group_blocks * block, hd)
        values = stored[:, :, hd:].reshape(group_blocks * block, hd).T
        live = [lax.rem(base + j - begin + n, n) < length for j in range(group_blocks)]
        for c in range(0, columns, column_chunk):
            span = slice(c, c + column_chunk)
            s = lax.dot_general(
                keys, rows[span, :], (((1,), (1,)), ((), ())), preferred_element_type=jnp.float32
            ) * scale
            before = top[:, span]
            m = before
            for j in range(group_blocks):
                peak = jnp.max(s[j * block:(j + 1) * block], axis=0, keepdims=True)
                m = jnp.maximum(m, jnp.where(live[j], peak, far_below))
            factor = jnp.exp2(before - m)
            parts = [
                jnp.exp2(s[j * block:(j + 1) * block] - jnp.where(live[j], m, far_above))
                for j in range(group_blocks)
            ]
            w = jnp.concatenate(parts, axis=0)
            top[:, span] = m
            total[:, span] = total[:, span] * factor + jnp.sum(w, axis=0, keepdims=True)
            acc[:, span] = acc[:, span] * factor + jnp.dot(
                values, w.astype(jnp.bfloat16), preferred_element_type=jnp.float32
            )

    for i in range(1, requests):
        new_arrival(i).wait_recv()
    for i in range(1, heads):
        chosen[i] = pick(other(me, i, n))
        pick_copy(i, head).start()
    store_ref[0, head] = pick(me)

    for d in range(1, group_blocks):
        block_arrival(other(me, d, n)).wait_recv()
    fold(lax.div(me, group_blocks) * group_blocks)

    @pl.loop(1, n // group_blocks)
    def _(i):
        base = other(lax.div(me, group_blocks), i, n // group_blocks) * group_blocks
        for j in range(group_blocks):
            block_arrival(base + j).wait_recv()
        fold(base)

    for h in range(groups):
        span = slice(h * block, (h + 1) * block)
        att_ref[0, :, h * hd:(h + 1) * hd] = (acc[:, span] / total[:, span]).T.astype(att_ref.dtype)

    for i in range(1, heads):
        pick_copy(i, lax.rem(other(me, i, n), heads)).wait_recv()
    for i in range(1, heads):
        pick_copy(i, head).wait_send()
    for i in range(1, requests):
        new_copy(i).wait_send()
    for d in order:
        block_copy(d).wait_send()


def on_device(n, queries, new_kv, pool_kv, hit_slots, prefix_blocks, new_owners):
    heads, block, width = pool_kv.shape[1:]
    requests = hit_slots.shape[0]
    hd = width // 2
    columns = queries.shape[2] // hd * block
    hbm, vmem = pl.BlockSpec(memory_space=pltpu.HBM), pl.BlockSpec(memory_space=pltpu.VMEM)
    slab = lambda k: pltpu.VMEM((k, block, width), pool_kv.dtype)
    dma = lambda k: pltpu.SemaphoreType.DMA((k,))
    keys = (n + 1) * block
    return pl.pallas_call(
        functools.partial(kernel, n),
        out_shape=(
            jax.ShapeDtypeStruct(queries.shape, queries.dtype),
            jax.ShapeDtypeStruct((1, heads, block, width), pool_kv.dtype),
        ),
        in_specs=[hbm] * 6,
        out_specs=(vmem, vmem),
        scratch_shapes=[
            pltpu.SMEM(hit_slots.shape, jnp.int32), pltpu.SMEM((1, requests), jnp.int32),
            pltpu.SMEM(new_owners.shape, jnp.int32),
            pltpu.VMEM(queries.shape, queries.dtype), pltpu.VMEM(new_kv.shape, new_kv.dtype),
            pltpu.VMEM(pool_kv.shape, pool_kv.dtype), dma(5 + pool_kv.shape[0]),
            slab(n), slab(n), slab(requests), slab(heads),
            pltpu.VMEM((columns, hd), jnp.bfloat16),
            pltpu.VMEM((hd, columns), jnp.float32),
            pltpu.VMEM((1, columns), jnp.float32),
            pltpu.VMEM((1, columns), jnp.float32),
            dma(n), dma(n), dma(requests), dma(requests), dma(heads), dma(heads),
        ],
        compiler_params=pltpu.CompilerParams(
            collective_id=0, has_side_effects=True, vmem_limit_bytes=56 * 2**20
        ),
        cost_estimate=pl.CostEstimate(
            flops=4 * columns * keys * hd,
            bytes_accessed=2 * (pool_kv.size + 2 * queries.size + 2 * heads * block * width),
            transcendentals=columns * keys,
        ),
    )(hit_slots, prefix_blocks[None], new_owners, queries, new_kv, pool_kv)


def solution(mesh):
    placed = (
        P(("grp", "pool"), None, None),
        P(("grp", "pool"), None, None),
        P(("grp", "pool"), None, None, None),
        P("grp", None),
        P("grp"),
        P("grp", None),
    )
    return jax.shard_map(
        functools.partial(on_device, mesh.shape["pool"]),
        mesh=mesh,
        in_specs=placed,
        out_specs=(P(("grp", "pool"), None, None), P(("grp", "pool"), None, None, None)),
        check_vma=False,
    )
```

```python
import functools
import math

import jax
import jax.numpy as jnp
from jax import lax
from jax.experimental import pallas as pl
from jax.experimental.pallas import tpu as pltpu
from jax.sharding import PartitionSpec as P

group_blocks = 2
column_chunk = 256
far_below = -1e30
far_above = 1e30
MESH = pl.DeviceIdType.MESH


def other(me, mask, n):
    out = 0
    bit = 1
    while bit < n:
        out = out + lax.rem(lax.div(me, bit) + (mask // bit if isinstance(mask, int) else lax.div(mask, bit)), 2) * bit
        bit *= 2
    return out


def kernel(
    n, hit_hbm, prefix_hbm, owner_hbm, q_hbm, new_hbm, pool_hbm, att_ref, store_ref,
    hit_ref, prefix_ref, owner_ref, q_ref, new_ref, pool_ref, in_sem, outgoing, fetched, gathered, chosen, rows, acc, top, total,
    send_sem, recv_sem, new_send, new_recv, pick_send, pick_recv,
):
    slots, heads, block, width = pool_ref.shape
    hd = width // 2
    requests, longest = hit_ref.shape
    groups = q_ref.shape[2] // hd
    columns = groups * block
    scale = math.log2(math.e) / math.sqrt(hd)
    me = lax.axis_index("pool")
    request, head = lax.div(me, heads), lax.rem(me, heads)

    loads = [
        pltpu.make_async_copy(hit_hbm, hit_ref, in_sem.at[0]),
        pltpu.make_async_copy(prefix_hbm, prefix_ref, in_sem.at[1]),
        pltpu.make_async_copy(owner_hbm, owner_ref, in_sem.at[2]),
        pltpu.make_async_copy(new_hbm, new_ref, in_sem.at[3]),
        pltpu.make_async_copy(q_hbm, q_ref, in_sem.at[4]),
    ] + [
        pltpu.make_async_copy(pool_hbm.at[k], pool_ref.at[k], in_sem.at[5 + k]) for k in range(slots)
    ]
    for load in loads:
        load.start()
    barrier = pltpu.get_barrier_semaphore()
    for d in range(1, n):
        pl.semaphore_signal(barrier, inc=1, device_id={"pool": other(me, d, n)}, device_id_type=MESH)

    def first_owner(r):
        return lax.div(hit_ref[r, 0], slots)

    def stage(target):
        r, g = lax.div(target, heads), lax.rem(target, heads)
        place = lax.rem(me - first_owner(r) + n, n)
        slot = lax.rem(hit_ref[r, jnp.minimum(place, longest - 1)], slots)
        return pool_ref[slot, g]

    def block_copy(d):
        target = other(me, d, n)
        return pltpu.make_async_remote_copy(
            src_ref=outgoing.at[target], dst_ref=fetched.at[me],
            send_sem=send_sem.at[target], recv_sem=recv_sem.at[me],
            device_id={"pool": target}, device_id_type=MESH,
        )

    def block_arrival(source):
        return pltpu.make_async_remote_copy(
            src_ref=outgoing.at[source], dst_ref=fetched.at[source],
            send_sem=send_sem.at[source], recv_sem=recv_sem.at[source],
            device_id={"pool": source}, device_id_type=MESH,
        )

    def new_copy(i):
        target = other(me, i * heads, n)
        return pltpu.make_async_remote_copy(
            src_ref=new_ref.at[0], dst_ref=gathered.at[request],
            send_sem=new_send.at[i], recv_sem=new_recv.at[request],
            device_id={"pool": target}, device_id_type=MESH,
        )

    def new_arrival(i):
        target = other(me, i * heads, n)
        r = lax.div(target, heads)
        return pltpu.make_async_remote_copy(
            src_ref=new_ref.at[0], dst_ref=gathered.at[r],
            send_sem=new_send.at[i], recv_sem=new_recv.at[r],
            device_id={"pool": target}, device_id_type=MESH,
        )

    def pick_copy(i, place):
        target = other(me, i, n)
        return pltpu.make_async_remote_copy(
            src_ref=chosen.at[i], dst_ref=store_ref.at[0, place],
            send_sem=pick_send.at[i], recv_sem=pick_recv.at[place],
            device_id={"pool": target}, device_id_type=MESH,
        )

    def pick(target):
        source, owned = 0, 0
        for r in range(requests):
            here = jnp.where((owner_ref[r, 0] == target) | (owner_ref[r, 1] == target), 1, 0)
            source = source + r * here
            owned = owned + here
        value = gathered[source]
        return jnp.where(owned > 0, value, jnp.zeros_like(value))

    for load in loads[:4] + loads[5:]:
        load.wait()
    order = []
    for i in range(n // 2):
        order += [n // 2 + i] + ([i + 1] if i + 1 < n // 2 else [])
    for d in order:
        target = other(me, d, n)
        outgoing[target] = stage(target)
    fetched[me] = stage(me)
    gathered[request] = new_ref[0]
    pl.semaphore_wait(barrier, n - 1)

    for i in range(1, requests):
        new_copy(i).start()
    for d in order:
        block_copy(d).start()

    loads[4].wait()
    for h in range(groups):
        rows[h * block:(h + 1) * block, :] = q_ref[0, :, h * hd:(h + 1) * hd]

    own_keys, own_values = new_ref[0, :, :hd], new_ref[0, :, hd:].T
    for c in range(0, columns, column_chunk):
        span = slice(c, c + column_chunk)
        s = lax.dot_general(
            own_keys, rows[span, :], (((1,), (1,)), ((), ())), preferred_element_type=jnp.float32
        ) * scale
        key_at = lax.broadcasted_iota(jnp.int32, s.shape, 0)
        token_at = lax.rem(lax.broadcasted_iota(jnp.int32, s.shape, 1), block)
        s = jnp.where(key_at <= token_at, s, far_below)
        m = jnp.max(s, axis=0, keepdims=True)
        w = jnp.where(key_at <= token_at, jnp.exp2(s - m), 0.0)
        top[:, span] = m
        total[:, span] = jnp.sum(w, axis=0, keepdims=True)
        acc[:, span] = jnp.dot(own_values, w.astype(jnp.bfloat16), preferred_element_type=jnp.float32)

    begin = first_owner(request)
    length = prefix_ref[0, request]

    def fold(base):
        stored = fetched.at[pl.ds(base, group_blocks)]
        keys = stored[:, :, :hd].reshape(group_blocks * block, hd)
        values = stored[:, :, hd:].reshape(group_blocks * block, hd).T
        live = [lax.rem(base + j - begin + n, n) < length for j in range(group_blocks)]
        for c in range(0, columns, column_chunk):
            span = slice(c, c + column_chunk)
            s = lax.dot_general(
                keys, rows[span, :], (((1,), (1,)), ((), ())), preferred_element_type=jnp.float32
            ) * scale
            before = top[:, span]
            m = before
            for j in range(group_blocks):
                peak = jnp.max(s[j * block:(j + 1) * block], axis=0, keepdims=True)
                m = jnp.maximum(m, jnp.where(live[j], peak, far_below))
            factor = jnp.exp2(before - m)
            parts = [
                jnp.exp2(s[j * block:(j + 1) * block] - jnp.where(live[j], m, far_above))
                for j in range(group_blocks)
            ]
            w = jnp.concatenate(parts, axis=0)
            top[:, span] = m
            total[:, span] = total[:, span] * factor + jnp.sum(w, axis=0, keepdims=True)
            acc[:, span] = acc[:, span] * factor + jnp.dot(
                values, w.astype(jnp.bfloat16), preferred_element_type=jnp.float32
            )

    for i in range(1, requests):
        new_arrival(i).wait_recv()
    for i in range(1, heads):
        chosen[i] = pick(other(me, i, n))
        pick_copy(i, head).start()
    store_ref[0, head] = pick(me)

    for d in range(1, group_blocks):
        block_arrival(other(me, d, n)).wait_recv()
    fold(lax.div(me, group_blocks) * group_blocks)

    @pl.loop(1, n // group_blocks)
    def _(i):
        base = other(lax.div(me, group_blocks), i, n // group_blocks) * group_blocks
        for j in range(group_blocks):
            block_arrival(base + j).wait_recv()
        fold(base)

    for h in range(groups):
        span = slice(h * block, (h + 1) * block)
        att_ref[0, :, h * hd:(h + 1) * hd] = (acc[:, span] / total[:, span]).T.astype(att_ref.dtype)

    for i in range(1, heads):
        pick_copy(i, lax.rem(other(me, i, n), heads)).wait_recv()
    for i in range(1, heads):
        pick_copy(i, head).wait_send()
    for i in range(1, requests):
        new_copy(i).wait_send()
    for d in order:
        block_copy(d).wait_send()


def settle(att_ref, store_ref, att_out, store_out, att_held, store_held, in_sem, out_sem):
    pieces = []
    for source, held, target in ((att_ref, att_held, att_out), (store_ref, store_held, store_out)):
        size = source.shape[1] // 4
        pieces += [tuple(x.at[0, pl.ds(k * size, size)] for x in (source, held, target)) for k in range(4)]
    loads = [pltpu.make_async_copy(x, y, in_sem.at[k]) for k, (x, y, _) in enumerate(pieces)]
    stores = [pltpu.make_async_copy(y, z, out_sem.at[k]) for k, (_, y, z) in enumerate(pieces)]
    for load in loads:
        load.start()
    for load, keep in zip(loads, stores):
        load.wait()
        keep.start()
    for keep in stores:
        keep.wait()


def on_device(n, queries, new_kv, pool_kv, hit_slots, prefix_blocks, new_owners):
    heads, block, width = pool_kv.shape[1:]
    requests = hit_slots.shape[0]
    hd = width // 2
    columns = queries.shape[2] // hd * block
    hbm, vmem = pl.BlockSpec(memory_space=pltpu.HBM), pl.BlockSpec(memory_space=pltpu.VMEM)
    slab = lambda k: pltpu.VMEM((k, block, width), pool_kv.dtype)
    dma = lambda k: pltpu.SemaphoreType.DMA((k,))
    keys = (n + 1) * block
    att, store = pl.pallas_call(
        functools.partial(kernel, n),
        out_shape=(
            jax.ShapeDtypeStruct(queries.shape, queries.dtype),
            jax.ShapeDtypeStruct((1, heads, block, width), pool_kv.dtype),
        ),
        in_specs=[hbm] * 6,
        out_specs=(vmem, vmem),
        scratch_shapes=[
            pltpu.SMEM(hit_slots.shape, jnp.int32), pltpu.SMEM((1, requests), jnp.int32),
            pltpu.SMEM(new_owners.shape, jnp.int32),
            pltpu.VMEM(queries.shape, queries.dtype), pltpu.VMEM(new_kv.shape, new_kv.dtype),
            pltpu.VMEM(pool_kv.shape, pool_kv.dtype), dma(5 + pool_kv.shape[0]),
            slab(n), slab(n), slab(requests), slab(heads),
            pltpu.VMEM((columns, hd), jnp.bfloat16),
            pltpu.VMEM((hd, columns), jnp.float32),
            pltpu.VMEM((1, columns), jnp.float32),
            pltpu.VMEM((1, columns), jnp.float32),
            dma(n), dma(n), dma(requests), dma(requests), dma(heads), dma(heads),
        ],
        compiler_params=pltpu.CompilerParams(
            collective_id=0, has_side_effects=True, vmem_limit_bytes=56 * 2**20
        ),
        cost_estimate=pl.CostEstimate(
            flops=4 * columns * keys * hd,
            bytes_accessed=2 * (pool_kv.size + 2 * queries.size + 2 * heads * block * width),
            transcendentals=columns * keys,
        ),
    )(hit_slots, prefix_blocks[None], new_owners, queries, new_kv, pool_kv)
    anywhere = pl.BlockSpec(memory_space=pl.ANY)
    return pl.pallas_call(
        settle,
        out_shape=tuple(jax.ShapeDtypeStruct(x.shape, x.dtype) for x in (att, store)),
        in_specs=[anywhere] * 2,
        out_specs=(hbm, hbm),
        scratch_shapes=[
            pltpu.VMEM(att.shape, att.dtype), pltpu.VMEM(store.shape, store.dtype), dma(8), dma(8)
        ],
    )(att, store)


def solution(mesh):
    placed = (
        P(("grp", "pool"), None, None),
        P(("grp", "pool"), None, None),
        P(("grp", "pool"), None, None, None),
        P("grp", None),
        P("grp"),
        P("grp", None),
    )
    return jax.shard_map(
        functools.partial(on_device, mesh.shape["pool"]),
        mesh=mesh,
        in_specs=placed,
        out_specs=(P(("grp", "pool"), None, None), P(("grp", "pool"), None, None, None)),
        check_vma=False,
    )
```

```python
import functools
import math

import jax
import jax.numpy as jnp
from jax import lax
from jax.experimental import pallas as pl
from jax.experimental.pallas import tpu as pltpu
from jax.sharding import PartitionSpec as P

group_blocks = 2
column_chunk = 128
far_below = -1e30
far_above = 1e30
MESH = pl.DeviceIdType.MESH


def other(me, mask, n):
    out = 0
    bit = 1
    while bit < n:
        out = out + lax.rem(lax.div(me, bit) + (mask // bit if isinstance(mask, int) else lax.div(mask, bit)), 2) * bit
        bit *= 2
    return out


def kernel(
    n, hit_hbm, prefix_hbm, owner_hbm, q_hbm, new_hbm, pool_hbm, att_ref, store_ref,
    hit_ref, prefix_ref, owner_ref, q_ref, new_ref, pool_ref, in_sem, outgoing, fetched, gathered, chosen, rows, acc, top, total,
    send_sem, recv_sem, new_send, new_recv, pick_send, pick_recv,
):
    slots, heads, block, width = pool_ref.shape
    hd = width // 2
    requests, longest = hit_ref.shape
    groups = q_ref.shape[2] // hd
    columns = groups * block
    scale = math.log2(math.e) / math.sqrt(hd)
    me = lax.axis_index("pool")
    request, head = lax.div(me, heads), lax.rem(me, heads)

    loads = [
        pltpu.make_async_copy(hit_hbm, hit_ref, in_sem.at[0]),
        pltpu.make_async_copy(prefix_hbm, prefix_ref, in_sem.at[1]),
        pltpu.make_async_copy(owner_hbm, owner_ref, in_sem.at[2]),
        pltpu.make_async_copy(new_hbm, new_ref, in_sem.at[3]),
        pltpu.make_async_copy(q_hbm, q_ref, in_sem.at[4]),
    ] + [
        pltpu.make_async_copy(pool_hbm.at[k], pool_ref.at[k], in_sem.at[5 + k]) for k in range(slots)
    ]
    for load in loads:
        load.start()
    barrier = pltpu.get_barrier_semaphore()
    for d in range(1, n):
        pl.semaphore_signal(barrier, inc=1, device_id={"pool": other(me, d, n)}, device_id_type=MESH)

    def first_owner(r):
        return lax.div(hit_ref[r, 0], slots)

    def stage(target):
        r, g = lax.div(target, heads), lax.rem(target, heads)
        place = lax.rem(me - first_owner(r) + n, n)
        slot = lax.rem(hit_ref[r, jnp.minimum(place, longest - 1)], slots)
        return pool_ref[slot, g]

    def block_copy(d):
        target = other(me, d, n)
        return pltpu.make_async_remote_copy(
            src_ref=outgoing.at[target], dst_ref=fetched.at[me],
            send_sem=send_sem.at[target], recv_sem=recv_sem.at[me],
            device_id={"pool": target}, device_id_type=MESH,
        )

    def block_arrival(source):
        return pltpu.make_async_remote_copy(
            src_ref=outgoing.at[source], dst_ref=fetched.at[source],
            send_sem=send_sem.at[source], recv_sem=recv_sem.at[source],
            device_id={"pool": source}, device_id_type=MESH,
        )

    def new_copy(i):
        target = other(me, i * heads, n)
        return pltpu.make_async_remote_copy(
            src_ref=new_ref.at[0], dst_ref=gathered.at[request],
            send_sem=new_send.at[i], recv_sem=new_recv.at[request],
            device_id={"pool": target}, device_id_type=MESH,
        )

    def new_arrival(i):
        target = other(me, i * heads, n)
        r = lax.div(target, heads)
        return pltpu.make_async_remote_copy(
            src_ref=new_ref.at[0], dst_ref=gathered.at[r],
            send_sem=new_send.at[i], recv_sem=new_recv.at[r],
            device_id={"pool": target}, device_id_type=MESH,
        )

    def pick_copy(i, place):
        target = other(me, i, n)
        return pltpu.make_async_remote_copy(
            src_ref=chosen.at[i], dst_ref=store_ref.at[0, place],
            send_sem=pick_send.at[i], recv_sem=pick_recv.at[place],
            device_id={"pool": target}, device_id_type=MESH,
        )

    def pick(target):
        source, owned = 0, 0
        for r in range(requests):
            here = jnp.where((owner_ref[r, 0] == target) | (owner_ref[r, 1] == target), 1, 0)
            source = source + r * here
            owned = owned + here
        value = gathered[source]
        return jnp.where(owned > 0, value, jnp.zeros_like(value))

    for load in loads[:4] + loads[5:]:
        load.wait()
    order = []
    for i in range(n // 2):
        order += [n // 2 + i] + ([i + 1] if i + 1 < n // 2 else [])
    for d in order:
        target = other(me, d, n)
        outgoing[target] = stage(target)
    fetched[me] = stage(me)
    gathered[request] = new_ref[0]
    pl.semaphore_wait(barrier, n - 1)

    for i in range(1, requests):
        new_copy(i).start()
    for d in order:
        block_copy(d).start()

    loads[4].wait()
    for h in range(groups):
        rows[h * block:(h + 1) * block, :] = q_ref[0, :, h * hd:(h + 1) * hd]

    own_keys, own_values = new_ref[0, :, :hd], new_ref[0, :, hd:].T
    for c in range(0, columns, column_chunk):
        span = slice(c, c + column_chunk)
        s = lax.dot_general(
            own_keys, rows[span, :], (((1,), (1,)), ((), ())), preferred_element_type=jnp.float32
        ) * scale
        key_at = lax.broadcasted_iota(jnp.int32, s.shape, 0)
        token_at = lax.rem(lax.broadcasted_iota(jnp.int32, s.shape, 1), block)
        s = jnp.where(key_at <= token_at, s, far_below)
        m = jnp.max(s, axis=0, keepdims=True)
        w = jnp.where(key_at <= token_at, jnp.exp2(s - m), 0.0)
        top[:, span] = m
        total[:, span] = jnp.sum(w, axis=0, keepdims=True)
        acc[:, span] = jnp.dot(own_values, w.astype(jnp.bfloat16), preferred_element_type=jnp.float32)

    begin = first_owner(request)
    length = prefix_ref[0, request]

    def fold(base):
        stored = fetched.at[pl.ds(base, group_blocks)]
        keys = stored[:, :, :hd].reshape(group_blocks * block, hd)
        values = stored[:, :, hd:].reshape(group_blocks * block, hd).T
        live = [lax.rem(base + j - begin + n, n) < length for j in range(group_blocks)]
        for c in range(0, columns, column_chunk):
            span = slice(c, c + column_chunk)
            s = lax.dot_general(
                keys, rows[span, :], (((1,), (1,)), ((), ())), preferred_element_type=jnp.float32
            ) * scale
            before = top[:, span]
            m = before
            for j in range(group_blocks):
                peak = jnp.max(s[j * block:(j + 1) * block], axis=0, keepdims=True)
                m = jnp.maximum(m, jnp.where(live[j], peak, far_below))
            factor = jnp.exp2(before - m)
            parts = [
                jnp.exp2(s[j * block:(j + 1) * block] - jnp.where(live[j], m, far_above))
                for j in range(group_blocks)
            ]
            w = jnp.concatenate(parts, axis=0)
            top[:, span] = m
            total[:, span] = total[:, span] * factor + jnp.sum(w, axis=0, keepdims=True)
            acc[:, span] = acc[:, span] * factor + jnp.dot(
                values, w.astype(jnp.bfloat16), preferred_element_type=jnp.float32
            )

    for i in range(1, requests):
        new_arrival(i).wait_recv()
    for i in range(1, heads):
        chosen[i] = pick(other(me, i, n))
        pick_copy(i, head).start()
    store_ref[0, head] = pick(me)

    for d in range(1, group_blocks):
        block_arrival(other(me, d, n)).wait_recv()
    fold(lax.div(me, group_blocks) * group_blocks)

    @pl.loop(1, n // group_blocks)
    def _(i):
        base = other(lax.div(me, group_blocks), i, n // group_blocks) * group_blocks
        for j in range(group_blocks):
            block_arrival(base + j).wait_recv()
        fold(base)

    for h in range(groups):
        span = slice(h * block, (h + 1) * block)
        att_ref[0, :, h * hd:(h + 1) * hd] = (acc[:, span] / total[:, span]).T.astype(att_ref.dtype)

    for i in range(1, heads):
        pick_copy(i, lax.rem(other(me, i, n), heads)).wait_recv()
    for i in range(1, heads):
        pick_copy(i, head).wait_send()
    for i in range(1, requests):
        new_copy(i).wait_send()
    for d in order:
        block_copy(d).wait_send()


def settle(att_ref, store_ref, att_out, store_out, att_held, store_held, in_sem, out_sem):
    pieces = []
    for source, held, target in ((att_ref, att_held, att_out), (store_ref, store_held, store_out)):
        size = source.shape[1] // 4
        pieces += [tuple(x.at[0, pl.ds(k * size, size)] for x in (source, held, target)) for k in range(4)]
    loads = [pltpu.make_async_copy(x, y, in_sem.at[k]) for k, (x, y, _) in enumerate(pieces)]
    stores = [pltpu.make_async_copy(y, z, out_sem.at[k]) for k, (_, y, z) in enumerate(pieces)]
    for load in loads:
        load.start()
    for load, keep in zip(loads, stores):
        load.wait()
        keep.start()
    for keep in stores:
        keep.wait()


def on_device(n, queries, new_kv, pool_kv, hit_slots, prefix_blocks, new_owners):
    heads, block, width = pool_kv.shape[1:]
    requests = hit_slots.shape[0]
    hd = width // 2
    columns = queries.shape[2] // hd * block
    hbm, vmem = pl.BlockSpec(memory_space=pltpu.HBM), pl.BlockSpec(memory_space=pltpu.VMEM)
    slab = lambda k: pltpu.VMEM((k, block, width), pool_kv.dtype)
    dma = lambda k: pltpu.SemaphoreType.DMA((k,))
    keys = (n + 1) * block
    att, store = pl.pallas_call(
        functools.partial(kernel, n),
        out_shape=(
            jax.ShapeDtypeStruct(queries.shape, queries.dtype),
            jax.ShapeDtypeStruct((1, heads, block, width), pool_kv.dtype),
        ),
        in_specs=[hbm] * 6,
        out_specs=(vmem, vmem),
        scratch_shapes=[
            pltpu.SMEM(hit_slots.shape, jnp.int32), pltpu.SMEM((1, requests), jnp.int32),
            pltpu.SMEM(new_owners.shape, jnp.int32),
            pltpu.VMEM(queries.shape, queries.dtype), pltpu.VMEM(new_kv.shape, new_kv.dtype),
            pltpu.VMEM(pool_kv.shape, pool_kv.dtype), dma(5 + pool_kv.shape[0]),
            slab(n), slab(n), slab(requests), slab(heads),
            pltpu.VMEM((columns, hd), jnp.bfloat16),
            pltpu.VMEM((hd, columns), jnp.float32),
            pltpu.VMEM((1, columns), jnp.float32),
            pltpu.VMEM((1, columns), jnp.float32),
            dma(n), dma(n), dma(requests), dma(requests), dma(heads), dma(heads),
        ],
        compiler_params=pltpu.CompilerParams(
            collective_id=0, has_side_effects=True, vmem_limit_bytes=56 * 2**20
        ),
        cost_estimate=pl.CostEstimate(
            flops=4 * columns * keys * hd,
            bytes_accessed=2 * (pool_kv.size + 2 * queries.size + 2 * heads * block * width),
            transcendentals=columns * keys,
        ),
    )(hit_slots, prefix_blocks[None], new_owners, queries, new_kv, pool_kv)
    anywhere = pl.BlockSpec(memory_space=pl.ANY)
    return pl.pallas_call(
        settle,
        out_shape=tuple(jax.ShapeDtypeStruct(x.shape, x.dtype) for x in (att, store)),
        in_specs=[anywhere] * 2,
        out_specs=(hbm, hbm),
        scratch_shapes=[
            pltpu.VMEM(att.shape, att.dtype), pltpu.VMEM(store.shape, store.dtype), dma(8), dma(8)
        ],
    )(att, store)


def solution(mesh):
    placed = (
        P(("grp", "pool"), None, None),
        P(("grp", "pool"), None, None),
        P(("grp", "pool"), None, None, None),
        P("grp", None),
        P("grp"),
        P("grp", None),
    )
    return jax.shard_map(
        functools.partial(on_device, mesh.shape["pool"]),
        mesh=mesh,
        in_specs=placed,
        out_specs=(P(("grp", "pool"), None, None), P(("grp", "pool"), None, None, None)),
        check_vma=False,
    )
```
